32 devices in a mesh: row: 8 (over z, x), col: 4 (over y, core).
Axes of the slice: x: 2, y: 2, z: 4, core: 2. Of those that a mesh axis runs over, the one named last changes fastest.
Arguments:
- flow: bfloat16 [2048, 2048], P('row', 'col'), may hold values from 0.0009994507 to 1
- pattern: int32 [8, 8], P('row', 'col'), may hold values 0 or 1
- keep: int32 [8, 8], P('row', 'col'), may hold values 0 or 1
Outputs:
- clustered: float32 [2048, 2048], P('row', 'col')
The draws below stay inside these ranges and needn't reach their ends.
All inputs are finite; a program needn't handle non-finite values. No bound on the sum of `pattern` or of `keep` on one device may be relied on, other than what follows from the above.
Results may differ from the reference program's by a relative error of at most 0.00046.
Values may be sent and summed in bfloat16 or wider, within the bound.
No kernel may reach another device: no remote copies, remote signals or barrier semaphores. Data moves between devices by JAX's collectives and lax.ppermute only.
A program may use at most 128 MiB of HBM per device.

```python
import math
import jax
import jax.numpy as jnp

TILE = 256
NT = 8
ORDER = 2048


def touch_ends(entries, key, low, high):
    index_at = [jax.random.randint(jax.random.fold_in(key, axis), (), 0, length) for axis, length in enumerate(entries.shape)]
    main_axis = entries.shape.index(max(entries.shape))
    beside = index_at[:main_axis] + [(index_at[main_axis] + 1) % entries.shape[main_axis]] + index_at[main_axis + 1:]
    return entries.at[tuple(index_at)].set(low).at[tuple(beside)].set(high)


def block_levels(rng, shape, split, least, top_value):
    level = 1.0
    for position, parts in split:
        draws = jax.random.uniform(jax.random.fold_in(jax.random.fold_in(rng, 6), position), (parts,), jnp.float32, least / len(split), top_value / len(split))
        level = level * jnp.repeat(jnp.exp(draws), shape[position] // parts).reshape((-1,) + (1,) * (len(shape) - 1 - position))
    return level


def setup_inputs(seed: int = 0) -> dict:
    key_list = jax.random.split(jax.random.key(seed), 4)
    return {
        "flow": jnp.clip(jnp.exp(math.log(1.0) - 6.9083047 * jax.random.uniform(key_list[0], (ORDER, ORDER), jnp.float32) ** block_levels(key_list[0], (ORDER, ORDER), ((0, 8), (1, 4)), -0.2, 0.2)), 0.0009994507, 1.0).astype(jnp.bfloat16),
        "pattern": touch_ends((jax.random.randint(key_list[1], (NT, NT), 0, 5) < 3).astype(jnp.int32), jax.random.fold_in(key_list[1], 1), 0, 1),
        "keep": touch_ends((jax.random.randint(key_list[2], (NT, NT), 0, 5) < 4).astype(jnp.int32), jax.random.fold_in(key_list[2], 1), 0, 1),
    }


def tile_mask(grid, tile):
    count = grid.shape[0]
    wide = jnp.broadcast_to(grid[:, None, :, None], (count, tile, count, tile))
    return wide.reshape(count * tile, count * tile)


def reference(flow, pattern, keep):
    order = ORDER
    loops = jnp.eye(order, dtype=jnp.float32)
    base = flow.astype(jnp.float32) * tile_mask((pattern > 0).astype(jnp.float32), TILE) + loops
    mass = jnp.sum(base, axis=0)
    stochastic = (base / mass[None, :]).astype(jnp.bfloat16)
    expanded = jnp.dot(stochastic, stochastic, preferred_element_type=jnp.float32)
    kept = jnp.logical_or(keep > 0, jnp.eye(NT, dtype=jnp.int32) > 0).astype(jnp.float32)
    expanded = expanded * tile_mask(kept, TILE)
    inflated = expanded * expanded
    totals = jnp.sum(inflated, axis=0)
    scale = order / totals
    return inflated * scale[None, :]
```

```python
import functools

import jax
import jax.numpy as jnp
from jax import lax
from jax.experimental import pallas as pl
from jax.experimental.pallas import tpu as pltpu
from jax.sharding import PartitionSpec as P

LANES = 128
VMEM = pltpu.VMEM
SMEM = pltpu.SMEM


def ring_order(count):
    return list(range(0, count, 2)) + list(range(count - 1, 0, -2))


def ring_position(index, count):
    return jnp.where(index % 2 == 0, index // 2, count - 1 - index // 2)


def ring_member(position, count):
    position = lax.rem(position + count, count)
    return jnp.where(position < count // 2, 2 * position, 2 * (count - 1 - position) + 1)


def identity(tile):
    rows = lax.broadcasted_iota(jnp.int32, (tile, tile), 0)
    return (rows == lax.broadcasted_iota(jnp.int32, (tile, tile), 1)).astype(jnp.float32)


def mask_kernel(flow_ref, pattern_ref, masked_ref, sums_ref):
    tile = flow_ref.shape[0]
    tcols = flow_ref.shape[1] // tile
    row, col = lax.axis_index("row"), lax.axis_index("col")
    for t in range(tcols):
        cut = slice(t * tile, (t + 1) * tile)
        listed = (pattern_ref[0, t] > 0).astype(jnp.float32)
        block = flow_ref[:, cut].astype(jnp.float32) * listed
        masked_ref[:, cut] = block.astype(jnp.bfloat16)
        loop = (col * tcols + t == row).astype(jnp.float32)
        sums_ref[:, cut] = jnp.sum(block, axis=0, keepdims=True) + loop


def store_normalized(place, block, inverse, is_diagonal):
    place[...] = (block[...].astype(jnp.float32) * inverse).astype(jnp.bfloat16)

    @pl.when(is_diagonal)
    def _():
        base = block[...].astype(jnp.float32) + identity(block.shape[0])
        place[...] = (base * inverse).astype(jnp.bfloat16)


def square_kernel(rows_n, cols_n, last, *refs):
    blocks, refs = refs[: rows_n - 1], refs[rows_n - 1 :]
    own_cols, refs = refs[:cols_n], refs[cols_n:]
    mate_cols, refs = refs[:cols_n], refs[cols_n:]
    masses, refs = refs[:cols_n], refs[cols_n:]
    chunk_mass, acc_ref, left_last_ref, left, right = refs
    step = pl.program_id(0)
    row, col = lax.axis_index("row"), lax.axis_index("col")
    position = ring_position(row, rows_n)
    mate = row ^ (rows_n // 2)
    tile, cols_dev = own_cols[0].shape
    tcols = cols_dev // tile
    width = acc_ref.shape[1]

    @pl.when(step == 0)
    def _():
        for q in range(cols_n):
            for t in range(tcols):
                cut = slice(t * tile, (t + 1) * tile)
                inverse = 1.0 / masses[q][:, cut]
                k = (col ^ q) * tcols + t
                slot = lax.rem(ring_position(k, rows_n) - position + rows_n, rows_n)
                lanes = pl.ds(pl.multiple_of(slot * tile, tile), tile)
                store_normalized(left.at[0:tile, lanes], own_cols[q].at[:, cut], inverse, k == row)
                store_normalized(left.at[tile : 2 * tile, lanes], mate_cols[q].at[:, cut], inverse, k == mate)
        left_last_ref[...] = left[:, last * tile : (last + 1) * tile]

    slots = [s for s in range(rows_n) if s != last]
    for slot, block in zip(slots, blocks):
        r = ring_member(position + slot, rows_n)
        for t in range(width // tile):
            cut = slice(t * tile, (t + 1) * tile)
            tile_col = col * tcols + step * (width // tile) + t
            store_normalized(
                right.at[slot * tile : (slot + 1) * tile, cut], block.at[:, cut], 1.0 / chunk_mass[:, cut], tile_col == r
            )
    group = 4
    pieces = [(a, min(a + group, last)) for a in range(0, last, group)]
    pieces += [(a, min(a + group, rows_n)) for a in range(last + 1, rows_n, group)]
    for number, (a, b) in enumerate(pieces):
        span = slice(a * tile, b * tile)
        product = jnp.dot(left[:, span], right[span, :], preferred_element_type=jnp.float32)
        acc_ref[...] = product if number == 0 else acc_ref[...] + product


def inflate_kernel(rows_n, last, acc_ref, left_ref, top_ref, bottom_ref, mass_ref, kept_ref, out_ref, tot_ref, right):
    step = pl.program_id(0)
    row, col = lax.axis_index("row"), lax.axis_index("col")
    r = ring_member(ring_position(row, rows_n) + last, rows_n)
    tile, width = out_ref.shape
    per_step = width // tile
    tcols = per_step * pl.num_programs(0)
    half = top_ref.shape[0]
    for t in range(per_step):
        cut = slice(t * tile, (t + 1) * tile)
        inverse = 1.0 / mass_ref[:, cut]
        right[0:half, cut] = (top_ref[:, cut].astype(jnp.float32) * inverse).astype(jnp.bfloat16)
        right[half:tile, cut] = (bottom_ref[:, cut].astype(jnp.float32) * inverse).astype(jnp.bfloat16)

        @pl.when(col * tcols + step * per_step + t == r)
        def _():
            eye = identity(tile)
            top = top_ref[:, cut].astype(jnp.float32) + eye[0:half]
            bottom = bottom_ref[:, cut].astype(jnp.float32) + eye[half:tile]
            right[0:half, cut] = (top * inverse).astype(jnp.bfloat16)
            right[half:tile, cut] = (bottom * inverse).astype(jnp.bfloat16)

    for t in range(per_step):
        cut = slice(t * tile, (t + 1) * tile)
        product = acc_ref[:, cut] + jnp.dot(left_ref[...], right[:, cut], preferred_element_type=jnp.float32)
        mine = product[0:tile] * kept_ref[0, step * per_step + t]
        mine = mine * mine
        out_ref[:, cut] = mine
        other = product[tile : 2 * tile] * kept_ref[1, step * per_step + t]
        tot_ref[:, cut] = jnp.sum(mine + other * other, axis=0, keepdims=True)


def whole(shape=None):
    return pl.BlockSpec(memory_space=VMEM) if shape is None else pl.BlockSpec(shape, lambda j: (0, 0), memory_space=VMEM)


def body(rows_n, cols_n, flow, pattern, keep):
    tile, cols_dev = flow.shape
    tcols = pattern.shape[1]
    row, col = lax.axis_index("row"), lax.axis_index("col")
    position = ring_position(row, rows_n)
    half_ring, quarter = rows_n // 2, rows_n // 4
    width = min(cols_dev, 2 * tile)
    grid = (cols_dev // width,)

    order = ring_order(rows_n)
    up = [(order[i], order[(i + 1) % rows_n]) for i in range(rows_n)]
    down = [(b, a) for a, b in up]

    def send(value, axis, count, bit):
        return lax.ppermute(value, axis, [(i, i ^ bit) for i in range(count)])

    def send_row(value, bit):
        return send(value, "row", rows_n, bit)

    def col_blocks(value):
        held = {0: value}
        bit = cols_n // 2
        while bit:
            held.update({q ^ bit: send(v, "col", cols_n, bit) for q, v in list(held.items())})
            bit //= 2
        return [held[q] for q in range(cols_n)]

    masked, mass = pl.pallas_call(
        mask_kernel,
        out_shape=(
            jax.ShapeDtypeStruct(flow.shape, jnp.bfloat16),
            jax.ShapeDtypeStruct((1, cols_dev), jnp.float32),
        ),
        in_specs=[whole(), pl.BlockSpec(memory_space=SMEM)],
        out_specs=(whole(), whole()),
        compiler_params=pltpu.CompilerParams(vmem_limit_bytes=8 * tile * cols_dev * 2),
    )(flow, pattern)

    ring = {0: masked}
    bits = [1 << b for b in range(rows_n.bit_length() - 1)]
    tile_col = col * tcols + lax.iota(jnp.int32, tcols)
    kept = jnp.logical_or(keep > 0, (tile_col == row)[None, :]).astype(jnp.float32)
    behind = ahead = masked
    own_cols = mate_cols = masses = None
    for s in range(1, half_ring):
        behind, ahead = lax.ppermute(behind, "row", up), lax.ppermute(ahead, "row", down)
        ring[s], ring[rows_n - s] = ahead, behind
        if s == 1:
            own_cols = col_blocks(masked)
        if bits:
            for bit in (bits[:2] if s == 1 else bits):
                if bit == half_ring:
                    pad = jnp.zeros((1, LANES - tcols), jnp.float32)
                    other = send_row(jnp.concatenate([mass, kept, pad], axis=1), bit)
                    mass = mass + other[:, :cols_dev]
                    kept = jnp.concatenate([kept, other[:, cols_dev : cols_dev + tcols]], axis=0)
                else:
                    mass = mass + send_row(mass, bit)
            bits = bits[2:] if s == 1 else []
        elif masses is None:
            masses = col_blocks(mass)
        if s == quarter:
            mate = jnp.where(position % half_ring < quarter, ring[quarter], ring[rows_n - quarter])
        if s == quarter + 1:
            mate_cols = col_blocks(mate)
        behind, ahead, mass = lax.optimization_barrier((behind, ahead, mass))
    half = tile // 2
    top = lax.ppermute(behind[:half], "row", up)
    bottom = lax.ppermute(ahead[half:], "row", down)

    blocks = [ring[o] for o in range(rows_n) if o != half_ring]
    col_block = pl.BlockSpec((tile, width), lambda j: (0, j), memory_space=VMEM)
    col_row = pl.BlockSpec((1, width), lambda j: (0, j), memory_space=VMEM)
    full = whole((tile, cols_dev))
    acc, left_last = pl.pallas_call(
        functools.partial(square_kernel, rows_n, cols_n, half_ring),
        grid=grid,
        out_shape=(
            jax.ShapeDtypeStruct((2 * tile, cols_dev), jnp.float32),
            jax.ShapeDtypeStruct((2 * tile, tile), jnp.bfloat16),
        ),
        in_specs=[col_block] * len(blocks) + [full] * (2 * cols_n) + [whole((1, cols_dev))] * cols_n + [col_row],
        out_specs=(
            pl.BlockSpec((2 * tile, width), lambda j: (0, j), memory_space=VMEM),
            whole((2 * tile, tile)),
        ),
        scratch_shapes=[
            VMEM((2 * tile, rows_n * tile), jnp.bfloat16),
            VMEM((rows_n * tile, width), jnp.bfloat16),
        ],
        cost_estimate=pl.CostEstimate(
            flops=4 * tile * tile * rows_n * cols_dev, bytes_accessed=24 * tile * cols_dev, transcendentals=0
        ),
        compiler_params=pltpu.CompilerParams(
            vmem_limit_bytes=(20 if rows_n * tile <= 2048 else 60) * 1024 * 1024
        ),
    )(*blocks, *own_cols, *mate_cols, *masses, mass)

    inflated, totals = pl.pallas_call(
        functools.partial(inflate_kernel, rows_n, half_ring),
        grid=grid,
        out_shape=(
            jax.ShapeDtypeStruct((tile, cols_dev), jnp.float32),
            jax.ShapeDtypeStruct((1, cols_dev), jnp.float32),
        ),
        in_specs=[
            pl.BlockSpec((2 * tile, width), lambda j: (0, j), memory_space=VMEM),
            whole((2 * tile, tile)),
            pl.BlockSpec((half, width), lambda j: (0, j), memory_space=VMEM),
            pl.BlockSpec((half, width), lambda j: (0, j), memory_space=VMEM),
            col_row,
            pl.BlockSpec(memory_space=SMEM),
        ],
        out_specs=(col_block, col_row),
        scratch_shapes=[VMEM((tile, width), jnp.bfloat16)],
        cost_estimate=pl.CostEstimate(
            flops=4 * tile * tile * cols_dev, bytes_accessed=16 * tile * cols_dev, transcendentals=0
        ),
        compiler_params=pltpu.CompilerParams(vmem_limit_bytes=16 * 1024 * 1024),
    )(acc, left_last, top, bottom, mass, kept)

    bit = 1
    while bit < half_ring:
        wide = 2 * bit < half_ring
        if wide:
            walk = [0, 2 * bit, 3 * bit, bit]
            turn = [(i, (i & ~(3 * bit)) | walk[(walk.index(i & (3 * bit)) + 1) % 4]) for i in range(rows_n)]
            back = [(b, a) for a, b in turn]
            across = [(i, i ^ (3 * bit)) for i in range(rows_n)]
            totals = totals + sum(lax.ppermute(totals, "row", p) for p in (turn, back, across))
        else:
            totals = totals + send_row(totals, bit)
        bit *= 4 if wide else 2
    return inflated * (rows_n * tile / totals)


def solution(mesh):
    return jax.shard_map(
        functools.partial(body, mesh.shape["row"], mesh.shape["col"]),
        mesh=mesh,
        in_specs=(P("row", "col"), P("row", "col"), P("row", "col")),
        out_specs=P("row", "col"),
        check_vma=False,
    )
```

```python
import functools

import jax
import jax.numpy as jnp
from jax import lax
from jax.experimental import pallas as pl
from jax.experimental.pallas import tpu as pltpu
from jax.sharding import PartitionSpec as P

LANES = 128


def ring_order(count):
    return list(range(0, count, 2)) + list(range(count - 1, 0, -2))


def ring_position(index, count):
    return jnp.where(index % 2 == 0, index // 2, count - 1 - index // 2)


def ring_member(position, count):
    position = lax.rem(position + count, count)
    return jnp.where(position < count // 2, 2 * position, 2 * (count - 1 - position) + 1)


def identity(tile):
    rows = lax.broadcasted_iota(jnp.int32, (tile, tile), 0)
    return (rows == lax.broadcasted_iota(jnp.int32, (tile, tile), 1)).astype(jnp.float32)


def lane(note, start, index):
    tail = note[:, start:]
    return jnp.sum(jnp.where(lax.broadcasted_iota(jnp.int32, tail.shape, 1) == index, tail, 0.0), axis=1, keepdims=True)


def mask_rows(note, start, rows_n, tcols, t, tile):
    tail = note[:, start:]
    shape = (rows_n, tail.shape[1])
    wanted = lax.broadcasted_iota(jnp.int32, shape, 0) * tcols + t
    chosen = jnp.where(lax.broadcasted_iota(jnp.int32, shape, 1) == wanted, tail, 0.0)
    return jnp.broadcast_to(jnp.sum(chosen, axis=1, keepdims=True), (rows_n, tile))


def note_kernel(rows_n, flow_hbm, pattern_hbm, keep_hbm, note_ref, flow_ref, pattern_ref, keep_ref, sems):
    pairs = ((flow_hbm, flow_ref), (pattern_hbm, pattern_ref), (keep_hbm, keep_ref))
    copies = [pltpu.make_async_copy(a, b, sems.at[i]) for i, (a, b) in enumerate(pairs)]
    for copy in copies:
        copy.start()
    for copy in copies:
        copy.wait()
    tile, cols_dev = flow_ref.shape
    tcols = cols_dev // tile
    row, col = lax.axis_index("row"), lax.axis_index("col")
    lanes = lax.broadcasted_iota(jnp.int32, (1, note_ref.shape[1] - cols_dev), 1)
    masks = jnp.zeros(lanes.shape, jnp.float32)
    for t in range(tcols):
        cut = slice(t * tile, (t + 1) * tile)
        loop = col * tcols + t == row
        listed = (pattern_ref[0, t] > 0).astype(jnp.float32)
        kept = jnp.logical_or(keep_ref[0, t] > 0, loop).astype(jnp.float32)
        sums = jnp.sum(flow_ref[:, cut].astype(jnp.float32), axis=0, keepdims=True)
        note_ref[:, cut] = sums * listed + loop.astype(jnp.float32)
        masks = jnp.where(lanes == row * tcols + t, listed, masks)
        masks = jnp.where(lanes == (rows_n + row) * tcols + t, kept, masks)
    note_ref[:, cols_dev:] = masks


def store_normalized(place, block, flag, inverse, is_diagonal):
    place[...] = (block[...].astype(jnp.float32) * (inverse * flag)).astype(jnp.bfloat16)

    @pl.when(is_diagonal)
    def _():
        base = block[...].astype(jnp.float32) * flag + identity(block.shape[0])
        place[...] = (base * inverse).astype(jnp.bfloat16)


def square_kernel(rows_n, cols_n, last, *refs):
    blocks, refs = refs[: rows_n - 1], refs[rows_n - 1 :]
    own_cols, refs = refs[:cols_n], refs[cols_n:]
    mate_cols, refs = refs[:cols_n], refs[cols_n:]
    notes, refs = refs[:cols_n], refs[cols_n:]
    acc_ref, left_last_ref, left, right, flags = refs
    step = pl.program_id(0)
    row, col = lax.axis_index("row"), lax.axis_index("col")
    position = ring_position(row, rows_n)
    mate = row ^ (rows_n // 2)
    tile, cols_dev = own_cols[0].shape
    tcols = cols_dev // tile
    width = acc_ref.shape[1]

    @pl.when(step == 0)
    def _():
        for q in range(cols_n):
            for t in range(tcols):
                flags[q * tcols + t] = mask_rows(notes[q], cols_dev, rows_n, tcols, t, tile)
        for q in range(cols_n):
            for t in range(tcols):
                cut = slice(t * tile, (t + 1) * tile)
                inverse = 1.0 / notes[q][:, cut]
                k = (col ^ q) * tcols + t
                slot = lax.rem(ring_position(k, rows_n) - position + rows_n, rows_n)
                lanes = pl.ds(pl.multiple_of(slot * tile, tile), tile)
                for half, cols, r in ((0, own_cols, row), (1, mate_cols, mate)):
                    flag = flags[q * tcols + t, pl.ds(r, 1), :]
                    place = left.at[half * tile : (half + 1) * tile, lanes]
                    store_normalized(place, cols[q].at[:, cut], flag, inverse, k == r)
        left_last_ref[...] = left[:, last * tile : (last + 1) * tile]

    slots = [s for s in range(rows_n) if s != last]
    for slot, block in zip(slots, blocks):
        r = ring_member(position + slot, rows_n)
        for t in range(width // tile):
            cut = slice(t * tile, (t + 1) * tile)
            tile_col = step * (width // tile) + t
            lanes = pl.ds(pl.multiple_of(tile_col * tile, tile), tile)
            place = right.at[slot * tile : (slot + 1) * tile, cut]
            flag = flags[tile_col, pl.ds(r, 1), :]
            store_normalized(place, block.at[:, cut], flag, 1.0 / notes[0][:, lanes], col * tcols + tile_col == r)
    group = 4
    pieces = [(a, min(a + group, last)) for a in range(0, last, group)]
    pieces += [(a, min(a + group, rows_n)) for a in range(last + 1, rows_n, group)]
    for number, (a, b) in enumerate(pieces):
        span = slice(a * tile, b * tile)
        product = jnp.dot(left[:, span], right[span, :], preferred_element_type=jnp.float32)
        acc_ref[...] = product if number == 0 else acc_ref[...] + product


def inflate_kernel(rows_n, last, acc_ref, left_ref, top_ref, bottom_ref, note_ref, out_ref, tot_ref, right):
    step = pl.program_id(0)
    row, col = lax.axis_index("row"), lax.axis_index("col")
    r = ring_member(ring_position(row, rows_n) + last, rows_n)
    tile, width = out_ref.shape
    per_step = width // tile
    tcols = per_step * pl.num_programs(0)
    cols_dev = tcols * tile
    half = top_ref.shape[0]
    for t in range(per_step):
        cut = slice(t * tile, (t + 1) * tile)
        tile_col = step * per_step + t
        flag = lane(note_ref, cols_dev, r * tcols + tile_col)
        inverse = 1.0 / note_ref[:, pl.ds(pl.multiple_of(tile_col * tile, tile), tile)]
        right[0:half, cut] = (top_ref[:, cut].astype(jnp.float32) * (inverse * flag)).astype(jnp.bfloat16)
        right[half:tile, cut] = (bottom_ref[:, cut].astype(jnp.float32) * (inverse * flag)).astype(jnp.bfloat16)

        @pl.when(col * tcols + tile_col == r)
        def _():
            eye = identity(tile)
            top = top_ref[:, cut].astype(jnp.float32) * flag + eye[0:half]
            bottom = bottom_ref[:, cut].astype(jnp.float32) * flag + eye[half:tile]
            right[0:half, cut] = (top * inverse).astype(jnp.bfloat16)
            right[half:tile, cut] = (bottom * inverse).astype(jnp.bfloat16)

    for t in range(per_step):
        cut = slice(t * tile, (t + 1) * tile)
        tile_col = step * per_step + t
        product = acc_ref[:, cut] + jnp.dot(left_ref[...], right[:, cut], preferred_element_type=jnp.float32)
        mine = product[0:tile] * lane(note_ref, cols_dev, (rows_n + row) * tcols + tile_col)
        mine = mine * mine
        out_ref[:, cut] = mine
        mate = row ^ (rows_n // 2)
        other = product[tile : 2 * tile] * lane(note_ref, cols_dev, (rows_n + mate) * tcols + tile_col)
        tot_ref[:, cut] = jnp.sum(mine + other * other, axis=0, keepdims=True)


def whole():
    return pl.BlockSpec(memory_space=pltpu.VMEM)


def fixed(shape):
    return pl.BlockSpec(shape, lambda j: (0, 0), memory_space=pltpu.VMEM)


def body(rows_n, cols_n, flow, pattern, keep):
    tile, cols_dev = flow.shape
    tcols = pattern.shape[1]
    row = lax.axis_index("row")
    position = ring_position(row, rows_n)
    half_ring, quarter = rows_n // 2, rows_n // 4
    width = min(cols_dev, 2 * tile)
    grid = (cols_dev // width,)
    small = rows_n * tile <= 2048

    order = ring_order(rows_n)
    up = [(order[i], order[(i + 1) % rows_n]) for i in range(rows_n)]
    down = [(b, a) for a, b in up]

    def send(value, axis, count, bit):
        return lax.ppermute(value, axis, [(i, i ^ bit) for i in range(count)])

    def send_row(value, bit):
        return send(value, "row", rows_n, bit)

    def finish_cols(own, other):
        held = {0: own, cols_n // 2: other}
        bit = cols_n // 4
        while bit:
            held.update({q ^ bit: send(v, "col", cols_n, bit) for q, v in list(held.items())})
            bit //= 2
        return [held[q] for q in range(cols_n)]

    def send_far_col(value):
        return send(value, "col", cols_n, cols_n // 2)

    lanes = -(-2 * rows_n * tcols // LANES) * LANES
    note = pl.pallas_call(
        functools.partial(note_kernel, rows_n),
        out_shape=jax.ShapeDtypeStruct((1, cols_dev + lanes), jnp.float32),
        in_specs=[pl.BlockSpec(memory_space=pltpu.HBM)] * 3,
        out_specs=whole(),
        scratch_shapes=[
            pltpu.VMEM(flow.shape, flow.dtype),
            pltpu.SMEM(pattern.shape, pattern.dtype),
            pltpu.SMEM(keep.shape, keep.dtype),
            pltpu.SemaphoreType.DMA((3,)),
        ],
        compiler_params=pltpu.CompilerParams(vmem_limit_bytes=8 * tile * cols_dev * 2),
    )(flow, pattern, keep)

    ring = {0: flow}
    behind = ahead = flow
    bit_count = rows_n.bit_length() - 1
    other_mate = None
    def send_both(value, bit):
        pairs = [(r * cols_n + c, (r ^ bit) * cols_n + (c ^ (cols_n // 2))) for r in range(rows_n) for c in range(cols_n)]
        return lax.ppermute(value, ("row", "col"), pairs)

    for s in range(1, half_ring):
        behind, ahead = lax.ppermute(behind, "row", up), lax.ppermute(ahead, "row", down)
        if s == 1:
            note = note + send_row(note, 1)
            mine = send_far_col(flow)
        elif s == 2:
            near, far = note + send_row(note, 2), send_far_col(note) + send_both(note, 2)
            note = jnp.concatenate([near, far], axis=0)
        elif s <= bit_count:
            note = note + send_row(note, 1 << (s - 1))
        if s == quarter + 1:
            other_mate = send_far_col(mate)
        if s <= bit_count:
            if s == 1:
                behind, ahead, note, mine = lax.optimization_barrier((behind, ahead, note, mine))
            else:
                behind, ahead, note = lax.optimization_barrier((behind, ahead, note))
        else:
            behind, ahead = lax.optimization_barrier((behind, ahead))
        ring[s], ring[rows_n - s] = ahead, behind
        if s == quarter:
            mate = jnp.where(position % half_ring < quarter, ahead, behind)
    beside_note = send(note, "col", cols_n, 1)
    half = tile // 2
    top = lax.ppermute(behind[:half], "row", up)
    bottom = lax.ppermute(ahead[half:], "row", down)
    notes = [note[:1], beside_note[:1], note[1:], beside_note[1:]]
    note = note[:1]
    own_cols = finish_cols(flow, mine)
    mate_cols = finish_cols(mate, other_mate)

    blocks = [ring[o] for o in range(rows_n) if o != half_ring]
    col_block = pl.BlockSpec((tile, width), lambda j: (0, j), memory_space=pltpu.VMEM)
    wide_block = pl.BlockSpec((2 * tile, width), lambda j: (0, j), memory_space=pltpu.VMEM)
    half_block = pl.BlockSpec((half, width), lambda j: (0, j), memory_space=pltpu.VMEM)
    acc, left_last = pl.pallas_call(
        functools.partial(square_kernel, rows_n, cols_n, half_ring),
        grid=grid,
        out_shape=(
            jax.ShapeDtypeStruct((2 * tile, cols_dev), jnp.float32),
            jax.ShapeDtypeStruct((2 * tile, tile), jnp.bfloat16),
        ),
        in_specs=[col_block] * len(blocks) + [fixed(v.shape) for v in own_cols + mate_cols + notes],
        out_specs=(wide_block, fixed((2 * tile, tile))),
        scratch_shapes=[
            pltpu.VMEM((2 * tile, rows_n * tile), jnp.bfloat16),
            pltpu.VMEM((rows_n * tile, width), jnp.bfloat16),
            pltpu.VMEM((cols_n * tcols, rows_n, tile), jnp.float32),
        ],
        cost_estimate=pl.CostEstimate(
            flops=4 * tile * tile * rows_n * cols_dev, bytes_accessed=24 * tile * cols_dev, transcendentals=0
        ),
        compiler_params=pltpu.CompilerParams(vmem_limit_bytes=(20 if small else 60) * 1024 * 1024),
    )(*blocks, *own_cols, *mate_cols, *notes)

    inflated, totals = pl.pallas_call(
        functools.partial(inflate_kernel, rows_n, half_ring),
        grid=grid,
        out_shape=(
            jax.ShapeDtypeStruct((tile, cols_dev), jnp.float32),
            jax.ShapeDtypeStruct((1, cols_dev), jnp.float32),
        ),
        in_specs=[wide_block, fixed((2 * tile, tile)), half_block, half_block, fixed(note.shape)],
        out_specs=(col_block, pl.BlockSpec((1, width), lambda j: (0, j), memory_space=pltpu.VMEM)),
        scratch_shapes=[pltpu.VMEM((tile, width), jnp.bfloat16)],
        cost_estimate=pl.CostEstimate(
            flops=4 * tile * tile * cols_dev, bytes_accessed=16 * tile * cols_dev, transcendentals=0
        ),
        compiler_params=pltpu.CompilerParams(vmem_limit_bytes=16 * 1024 * 1024),
    )(acc, left_last, top, bottom, note)

    bit = 1
    while bit < half_ring:
        totals = totals + send_row(totals, bit)
        bit *= 2
    return inflated * (rows_n * tile / totals)


def solution(mesh):
    return jax.shard_map(
        functools.partial(body, mesh.shape["row"], mesh.shape["col"]),
        mesh=mesh,
        in_specs=(P("row", "col"), P("row", "col"), P("row", "col")),
        out_specs=P("row", "col"),
        check_vma=False,
    )
```

```python
import functools

import jax
import jax.numpy as jnp
from jax import lax
from jax.experimental import pallas as pl
from jax.experimental.pallas import tpu as pltpu
from jax.sharding import PartitionSpec as P

LANES = 128


def ring_order(count):
    return list(range(0, count, 2)) + list(range(count - 1, 0, -2))


def ring_position(index, count):
    return jnp.where(index % 2 == 0, index // 2, count - 1 - index // 2)


def ring_member(position, count):
    position = lax.rem(position + count, count)
    return jnp.where(position < count // 2, 2 * position, 2 * (count - 1 - position) + 1)


def identity(tile):
    rows = lax.broadcasted_iota(jnp.int32, (tile, tile), 0)
    return (rows == lax.broadcasted_iota(jnp.int32, (tile, tile), 1)).astype(jnp.float32)


def lane(note, start, index):
    tail = note[:, start:]
    return jnp.sum(jnp.where(lax.broadcasted_iota(jnp.int32, tail.shape, 1) == index, tail, 0.0), axis=1, keepdims=True)


def mask_rows(note, start, rows_n, tcols, t, tile):
    tail = note[:, start:]
    shape = (rows_n, tail.shape[1])
    wanted = lax.broadcasted_iota(jnp.int32, shape, 0) * tcols + t
    chosen = jnp.where(lax.broadcasted_iota(jnp.int32, shape, 1) == wanted, tail, 0.0)
    return jnp.broadcast_to(jnp.sum(chosen, axis=1, keepdims=True), (rows_n, tile))


def note_kernel(rows_n, flow_hbm, pattern_hbm, keep_hbm, note_ref, flow_ref, pattern_ref, keep_ref, sems):
    pairs = ((flow_hbm, flow_ref), (pattern_hbm, pattern_ref), (keep_hbm, keep_ref))
    copies = [pltpu.make_async_copy(a, b, sems.at[i]) for i, (a, b) in enumerate(pairs)]
    for copy in copies:
        copy.start()
    for copy in copies:
        copy.wait()
    tile, cols_dev = flow_ref.shape
    tcols = cols_dev // tile
    row, col = lax.axis_index("row"), lax.axis_index("col")
    lanes = lax.broadcasted_iota(jnp.int32, (1, note_ref.shape[1] - cols_dev), 1)
    masks = jnp.zeros(lanes.shape, jnp.float32)
    for t in range(tcols):
        cut = slice(t * tile, (t + 1) * tile)
        loop = col * tcols + t == row
        listed = (pattern_ref[0, t] > 0).astype(jnp.float32)
        kept = jnp.logical_or(keep_ref[0, t] > 0, loop).astype(jnp.float32)
        sums = jnp.sum(flow_ref[:, cut].astype(jnp.float32), axis=0, keepdims=True)
        note_ref[:, cut] = sums * listed + loop.astype(jnp.float32)
        masks = jnp.where(lanes == row * tcols + t, listed, masks)
        masks = jnp.where(lanes == (rows_n + row) * tcols + t, kept, masks)
    note_ref[:, cols_dev:] = masks


def store_normalized(place, block, flag, inverse, is_diagonal):
    place[...] = (block[...].astype(jnp.float32) * (inverse * flag)).astype(jnp.bfloat16)

    @pl.when(is_diagonal)
    def _():
        base = block[...].astype(jnp.float32) * flag + identity(block.shape[0])
        place[...] = (base * inverse).astype(jnp.bfloat16)


def square_kernel(rows_n, cols_n, last, *refs):
    blocks, refs = refs[: rows_n - 1], refs[rows_n - 1 :]
    own_cols, refs = refs[:cols_n], refs[cols_n:]
    mate_cols, refs = refs[:cols_n], refs[cols_n:]
    notes, refs = refs[:cols_n], refs[cols_n:]
    acc_ref, left_last_ref, left, right, flags = refs
    step = pl.program_id(0)
    row, col = lax.axis_index("row"), lax.axis_index("col")
    position = ring_position(row, rows_n)
    mate = row ^ (rows_n // 2)
    tile, cols_dev = own_cols[0].shape
    tcols = cols_dev // tile
    width = acc_ref.shape[1]

    @pl.when(step == 0)
    def _():
        for q in range(cols_n):
            for t in range(tcols):
                flags[q * tcols + t] = mask_rows(notes[q], cols_dev, rows_n, tcols, t, tile)
        for q in range(cols_n):
            for t in range(tcols):
                cut = slice(t * tile, (t + 1) * tile)
                inverse = 1.0 / notes[q][:, cut]
                k = (col ^ q) * tcols + t
                slot = lax.rem(ring_position(k, rows_n) - position + rows_n, rows_n)
                lanes = pl.ds(pl.multiple_of(slot * tile, tile), tile)
                for half, cols, r in ((0, own_cols, row), (1, mate_cols, mate)):
                    flag = flags[q * tcols + t, pl.ds(r, 1), :]
                    place = left.at[half * tile : (half + 1) * tile, lanes]
                    store_normalized(place, cols[q].at[:, cut], flag, inverse, k == r)
        left_last_ref[...] = left[:, last * tile : (last + 1) * tile]

    slots = [s for s in range(rows_n) if s != last]
    for slot, block in zip(slots, blocks):
        r = ring_member(position + slot, rows_n)
        for t in range(width // tile):
            cut = slice(t * tile, (t + 1) * tile)
            tile_col = step * (width // tile) + t
            lanes = pl.ds(pl.multiple_of(tile_col * tile, tile), tile)
            place = right.at[slot * tile : (slot + 1) * tile, cut]
            flag = flags[tile_col, pl.ds(r, 1), :]
            store_normalized(place, block.at[:, cut], flag, 1.0 / notes[0][:, lanes], col * tcols + tile_col == r)
    group = 4
    pieces = [(a, min(a + group, last)) for a in range(0, last, group)]
    pieces += [(a, min(a + group, rows_n)) for a in range(last + 1, rows_n, group)]
    for number, (a, b) in enumerate(pieces):
        span = slice(a * tile, b * tile)
        product = jnp.dot(left[:, span], right[span, :], preferred_element_type=jnp.float32)
        acc_ref[...] = product if number == 0 else acc_ref[...] + product


def inflate_kernel(rows_n, last, acc_ref, left_ref, top_ref, bottom_ref, note_ref, out_ref, tot_ref, right):
    step = pl.program_id(0)
    row, col = lax.axis_index("row"), lax.axis_index("col")
    r = ring_member(ring_position(row, rows_n) + last, rows_n)
    tile, width = out_ref.shape
    per_step = width // tile
    tcols = per_step * pl.num_programs(0)
    cols_dev = tcols * tile
    half = top_ref.shape[0]
    for t in range(per_step):
        cut = slice(t * tile, (t + 1) * tile)
        tile_col = step * per_step + t
        flag = lane(note_ref, cols_dev, r * tcols + tile_col)
        inverse = 1.0 / note_ref[:, pl.ds(pl.multiple_of(tile_col * tile, tile), tile)]
        right[0:half, cut] = (top_ref[:, cut].astype(jnp.float32) * (inverse * flag)).astype(jnp.bfloat16)
        right[half:tile, cut] = (bottom_ref[:, cut].astype(jnp.float32) * (inverse * flag)).astype(jnp.bfloat16)

        @pl.when(col * tcols + tile_col == r)
        def _():
            eye = identity(tile)
            top = top_ref[:, cut].astype(jnp.float32) * flag + eye[0:half]
            bottom = bottom_ref[:, cut].astype(jnp.float32) * flag + eye[half:tile]
            right[0:half, cut] = (top * inverse).astype(jnp.bfloat16)
            right[half:tile, cut] = (bottom * inverse).astype(jnp.bfloat16)

    for t in range(per_step):
        cut = slice(t * tile, (t + 1) * tile)
        tile_col = step * per_step + t
        product = acc_ref[:, cut] + jnp.dot(left_ref[...], right[:, cut], preferred_element_type=jnp.float32)
        mine = product[0:tile] * lane(note_ref, cols_dev, (rows_n + row) * tcols + tile_col)
        mine = mine * mine
        out_ref[:, cut] = mine
        mate = row ^ (rows_n // 2)
        other = product[tile : 2 * tile] * lane(note_ref, cols_dev, (rows_n + mate) * tcols + tile_col)
        tot_ref[:, cut] = jnp.sum(mine + other * other, axis=0, keepdims=True)


def whole():
    return pl.BlockSpec(memory_space=pltpu.VMEM)


def fixed(shape):
    return pl.BlockSpec(shape, lambda j: (0, 0), memory_space=pltpu.VMEM)


def body(rows_n, cols_n, flow, pattern, keep):
    tile, cols_dev = flow.shape
    tcols = pattern.shape[1]
    row = lax.axis_index("row")
    position = ring_position(row, rows_n)
    half_ring, quarter = rows_n // 2, rows_n // 4
    width = min(cols_dev, 2 * tile)
    grid = (cols_dev // width,)
    small = rows_n * tile <= 2048

    order = ring_order(rows_n)
    up = [(order[i], order[(i + 1) % rows_n]) for i in range(rows_n)]
    down = [(b, a) for a, b in up]

    def send(value, axis, count, bit):
        return lax.ppermute(value, axis, [(i, i ^ bit) for i in range(count)])

    def send_row(value, bit):
        return send(value, "row", rows_n, bit)

    def finish_cols(own, other):
        held = {0: own, cols_n // 2: other}
        bit = cols_n // 4
        while bit:
            held.update({q ^ bit: send(v, "col", cols_n, bit) for q, v in list(held.items())})
            bit //= 2
        return [held[q] for q in range(cols_n)]

    def send_far_col(value):
        return send(value, "col", cols_n, cols_n // 2)

    lanes = -(-2 * rows_n * tcols // LANES) * LANES
    note = pl.pallas_call(
        functools.partial(note_kernel, rows_n),
        out_shape=jax.ShapeDtypeStruct((1, cols_dev + lanes), jnp.float32),
        in_specs=[pl.BlockSpec(memory_space=pltpu.HBM)] * 3,
        out_specs=whole(),
        scratch_shapes=[
            pltpu.VMEM(flow.shape, flow.dtype),
            pltpu.SMEM(pattern.shape, pattern.dtype),
            pltpu.SMEM(keep.shape, keep.dtype),
            pltpu.SemaphoreType.DMA((3,)),
        ],
        compiler_params=pltpu.CompilerParams(vmem_limit_bytes=8 * tile * cols_dev * 2),
    )(flow, pattern, keep)

    def send_both(value, bit):
        pairs = [(r * cols_n + c, (r ^ bit) * cols_n + (c ^ (cols_n // 2))) for r in range(rows_n) for c in range(cols_n)]
        return lax.ppermute(value, ("row", "col"), pairs)

    ring = {0: flow}
    behind = ahead = flow
    bits = [1 << b for b in range(rows_n.bit_length() - 1)]
    bits[:2] = bits[1::-1]
    for s in range(1, half_ring):
        behind, ahead = lax.ppermute(behind, "row", up), lax.ppermute(ahead, "row", down)
        if s == 2:
            near, far = note + send_row(note, bits[1]), send_far_col(note) + send_both(note, bits[1])
            note = jnp.concatenate([near, far], axis=0)
        elif s <= len(bits):
            note = note + send_row(note, bits[s - 1])
        if s == 1:
            mine = send_far_col(flow)
            behind, ahead, note, mine = lax.optimization_barrier((behind, ahead, note, mine))
        else:
            behind, ahead, note = lax.optimization_barrier((behind, ahead, note))
        ring[s], ring[rows_n - s] = ahead, behind
        if s == quarter:
            mate = jnp.where(position % half_ring < quarter, ahead, behind)
            other_mate = send_far_col(mate)
    beside_note = send(note, "col", cols_n, 1)
    half = tile // 2
    top = lax.ppermute(behind[:half], "row", up)
    bottom = lax.ppermute(ahead[half:], "row", down)
    notes = [note[:1], beside_note[:1], note[1:], beside_note[1:]]
    note = note[:1]
    own_cols = finish_cols(flow, mine)
    mate_cols = finish_cols(mate, other_mate)

    blocks = [ring[o] for o in range(rows_n) if o != half_ring]
    col_block = pl.BlockSpec((tile, width), lambda j: (0, j), memory_space=pltpu.VMEM)
    wide_block = pl.BlockSpec((2 * tile, width), lambda j: (0, j), memory_space=pltpu.VMEM)
    half_block = pl.BlockSpec((half, width), lambda j: (0, j), memory_space=pltpu.VMEM)
    acc, left_last = pl.pallas_call(
        functools.partial(square_kernel, rows_n, cols_n, half_ring),
        grid=grid,
        out_shape=(
            jax.ShapeDtypeStruct((2 * tile, cols_dev), jnp.float32),
            jax.ShapeDtypeStruct((2 * tile, tile), jnp.bfloat16),
        ),
        in_specs=[col_block] * len(blocks) + [fixed(v.shape) for v in own_cols + mate_cols + notes],
        out_specs=(wide_block, fixed((2 * tile, tile))),
        scratch_shapes=[
            pltpu.VMEM((2 * tile, rows_n * tile), jnp.bfloat16),
            pltpu.VMEM((rows_n * tile, width), jnp.bfloat16),
            pltpu.VMEM((cols_n * tcols, rows_n, tile), jnp.float32),
        ],
        cost_estimate=pl.CostEstimate(
            flops=4 * tile * tile * rows_n * cols_dev, bytes_accessed=24 * tile * cols_dev, transcendentals=0
        ),
        compiler_params=pltpu.CompilerParams(vmem_limit_bytes=(20 if small else 60) * 1024 * 1024),
    )(*blocks, *own_cols, *mate_cols, *notes)

    inflated, totals = pl.pallas_call(
        functools.partial(inflate_kernel, rows_n, half_ring),
        grid=grid,
        out_shape=(
            jax.ShapeDtypeStruct((tile, cols_dev), jnp.float32),
            jax.ShapeDtypeStruct((1, cols_dev), jnp.float32),
        ),
        in_specs=[wide_block, fixed((2 * tile, tile)), half_block, half_block, fixed(note.shape)],
        out_specs=(col_block, pl.BlockSpec((1, width), lambda j: (0, j), memory_space=pltpu.VMEM)),
        scratch_shapes=[pltpu.VMEM((tile, width), jnp.bfloat16)],
        cost_estimate=pl.CostEstimate(
            flops=4 * tile * tile * cols_dev, bytes_accessed=16 * tile * cols_dev, transcendentals=0
        ),
        compiler_params=pltpu.CompilerParams(vmem_limit_bytes=16 * 1024 * 1024),
    )(acc, left_last, top, bottom, note)

    bit = 1
    while bit < half_ring:
        totals = totals + send_row(totals, bit)
        bit *= 2
    return inflated * (rows_n * tile / totals)


def solution(mesh):
    return jax.shard_map(
        functools.partial(body, mesh.shape["row"], mesh.shape["col"]),
        mesh=mesh,
        in_specs=(P("row", "col"), P("row", "col"), P("row", "col")),
        out_specs=P("row", "col"),
        check_vma=False,
    )
```

```python
import functools

import jax
import jax.numpy as jnp
from jax import lax
from jax.experimental import pallas as pl
from jax.experimental.pallas import tpu as pltpu
from jax.sharding import PartitionSpec as P

LANES = 128


def ring_order(count):
    return list(range(0, count, 2)) + list(range(count - 1, 0, -2))


def ring_position(index, count):
    return jnp.where(index % 2 == 0, index // 2, count - 1 - index // 2)


def ring_member(position, count):
    position = lax.rem(position + count, count)
    return jnp.where(position < count // 2, 2 * position, 2 * (count - 1 - position) + 1)


def identity(tile):
    rows = lax.broadcasted_iota(jnp.int32, (tile, tile), 0)
    return (rows == lax.broadcasted_iota(jnp.int32, (tile, tile), 1)).astype(jnp.float32)


def lane(note, start, index):
    tail = note[:, start:]
    return jnp.sum(jnp.where(lax.broadcasted_iota(jnp.int32, tail.shape, 1) == index, tail, 0.0), axis=1, keepdims=True)


def mask_rows(note, start, rows_n, tcols, t, tile):
    tail = note[:, start:]
    shape = (rows_n, tail.shape[1])
    wanted = lax.broadcasted_iota(jnp.int32, shape, 0) * tcols + t
    chosen = jnp.where(lax.broadcasted_iota(jnp.int32, shape, 1) == wanted, tail, 0.0)
    return jnp.broadcast_to(jnp.sum(chosen, axis=1, keepdims=True), (rows_n, tile))


def note_kernel(rows_n, flow_hbm, pattern_hbm, keep_hbm, note_ref, flow_ref, pattern_ref, keep_ref, sems):
    pairs = ((flow_hbm, flow_ref), (pattern_hbm, pattern_ref), (keep_hbm, keep_ref))
    copies = [pltpu.make_async_copy(a, b, sems.at[i]) for i, (a, b) in enumerate(pairs)]
    for copy in copies:
        copy.start()
    for copy in copies:
        copy.wait()
    tile, cols_dev = flow_ref.shape
    tcols = cols_dev // tile
    row, col = lax.axis_index("row"), lax.axis_index("col")
    lanes = lax.broadcasted_iota(jnp.int32, (1, note_ref.shape[1] - cols_dev), 1)
    masks = jnp.zeros(lanes.shape, jnp.float32)
    for t in range(tcols):
        cut = slice(t * tile, (t + 1) * tile)
        loop = col * tcols + t == row
        listed = (pattern_ref[0, t] > 0).astype(jnp.float32)
        kept = jnp.logical_or(keep_ref[0, t] > 0, loop).astype(jnp.float32)
        sums = jnp.sum(flow_ref[:, cut].astype(jnp.float32), axis=0, keepdims=True)
        note_ref[:, cut] = sums * listed + loop.astype(jnp.float32)
        masks = jnp.where(lanes == row * tcols + t, listed, masks)
        masks = jnp.where(lanes == (rows_n + row) * tcols + t, kept, masks)
    note_ref[:, cols_dev:] = masks


def store_normalized(place, block, flag, inverse, is_diagonal):
    place[...] = (block[...].astype(jnp.float32) * (inverse * flag)).astype(jnp.bfloat16)

    @pl.when(is_diagonal)
    def _():
        base = block[...].astype(jnp.float32) * flag + identity(block.shape[0])
        place[...] = (base * inverse).astype(jnp.bfloat16)


def square_kernel(rows_n, cols_n, last, *refs):
    blocks, refs = refs[: rows_n - 1], refs[rows_n - 1 :]
    own_cols, refs = refs[:cols_n], refs[cols_n:]
    mate_cols, refs = refs[:cols_n], refs[cols_n:]
    notes, refs = refs[:cols_n], refs[cols_n:]
    acc_ref, left_last_ref, left, right, flags = refs
    step = pl.program_id(0)
    row, col = lax.axis_index("row"), lax.axis_index("col")
    position = ring_position(row, rows_n)
    mate = row ^ (rows_n // 2)
    tile, cols_dev = own_cols[0].shape
    tcols = cols_dev // tile
    width = acc_ref.shape[1]

    @pl.when(step == 0)
    def _():
        for q in range(cols_n):
            for t in range(tcols):
                flags[q * tcols + t] = mask_rows(notes[q], cols_dev, rows_n, tcols, t, tile)
        for q in range(cols_n):
            for t in range(tcols):
                cut = slice(t * tile, (t + 1) * tile)
                inverse = 1.0 / notes[q][:, cut]
                k = (col ^ q) * tcols + t
                slot = lax.rem(ring_position(k, rows_n) - position + rows_n, rows_n)
                lanes = pl.ds(pl.multiple_of(slot * tile, tile), tile)
                for half, cols, r in ((0, own_cols, row), (1, mate_cols, mate)):
                    flag = flags[q * tcols + t, pl.ds(r, 1), :]
                    place = left.at[half * tile : (half + 1) * tile, lanes]
                    store_normalized(place, cols[q].at[:, cut], flag, inverse, k == r)
        left_last_ref[...] = left[:, last * tile : (last + 1) * tile]

    slots = [s for s in range(rows_n) if s != last]
    for slot, block in zip(slots, blocks):
        r = ring_member(position + slot, rows_n)
        for t in range(width // tile):
            cut = slice(t * tile, (t + 1) * tile)
            tile_col = step * (width // tile) + t
            lanes = pl.ds(pl.multiple_of(tile_col * tile, tile), tile)
            place = right.at[slot * tile : (slot + 1) * tile, cut]
            flag = flags[tile_col, pl.ds(r, 1), :]
            store_normalized(place, block.at[:, cut], flag, 1.0 / notes[0][:, lanes], col * tcols + tile_col == r)
    group = 4
    pieces = [(a, min(a + group, last)) for a in range(0, last, group)]
    pieces += [(a, min(a + group, rows_n)) for a in range(last + 1, rows_n, group)]
    for number, (a, b) in enumerate(pieces):
        span = slice(a * tile, b * tile)
        product = jnp.dot(left[:, span], right[span, :], preferred_element_type=jnp.float32)
        acc_ref[...] = product if number == 0 else acc_ref[...] + product


def inflate_kernel(rows_n, last, acc_ref, left_ref, top_ref, bottom_ref, note_ref, out_ref, tot_ref, right):
    step = pl.program_id(0)
    row, col = lax.axis_index("row"), lax.axis_index("col")
    r = ring_member(ring_position(row, rows_n) + last, rows_n)
    tile, width = out_ref.shape
    per_step = width // tile
    tcols = per_step * pl.num_programs(0)
    cols_dev = tcols * tile
    half = top_ref.shape[0]
    for t in range(per_step):
        cut = slice(t * tile, (t + 1) * tile)
        tile_col = step * per_step + t
        flag = lane(note_ref, cols_dev, r * tcols + tile_col)
        inverse = 1.0 / note_ref[:, pl.ds(pl.multiple_of(tile_col * tile, tile), tile)]
        right[0:half, cut] = (top_ref[:, cut].astype(jnp.float32) * (inverse * flag)).astype(jnp.bfloat16)
        right[half:tile, cut] = (bottom_ref[:, cut].astype(jnp.float32) * (inverse * flag)).astype(jnp.bfloat16)

        @pl.when(col * tcols + tile_col == r)
        def _():
            eye = identity(tile)
            top = top_ref[:, cut].astype(jnp.float32) * flag + eye[0:half]
            bottom = bottom_ref[:, cut].astype(jnp.float32) * flag + eye[half:tile]
            right[0:half, cut] = (top * inverse).astype(jnp.bfloat16)
            right[half:tile, cut] = (bottom * inverse).astype(jnp.bfloat16)

    for t in range(per_step):
        cut = slice(t * tile, (t + 1) * tile)
        tile_col = step * per_step + t
        product = acc_ref[:, cut] + jnp.dot(left_ref[...], right[:, cut], preferred_element_type=jnp.float32)
        mine = product[0:tile] * lane(note_ref, cols_dev, (rows_n + row) * tcols + tile_col)
        mine = mine * mine
        out_ref[:, cut] = mine
        mate = row ^ (rows_n // 2)
        other = product[tile : 2 * tile] * lane(note_ref, cols_dev, (rows_n + mate) * tcols + tile_col)
        tot_ref[:, cut] = jnp.sum(mine + other * other, axis=0, keepdims=True)


def whole():
    return pl.BlockSpec(memory_space=pltpu.VMEM)


def fixed(shape):
    return pl.BlockSpec(shape, lambda j: (0, 0), memory_space=pltpu.VMEM)


def body(rows_n, cols_n, flow, pattern, keep):
    tile, cols_dev = flow.shape
    tcols = pattern.shape[1]
    row = lax.axis_index("row")
    position = ring_position(row, rows_n)
    half_ring, quarter = rows_n // 2, rows_n // 4
    width = min(cols_dev, 2 * tile)
    grid = (cols_dev // width,)
    small = rows_n * tile <= 2048

    order = ring_order(rows_n)
    up = [(order[i], order[(i + 1) % rows_n]) for i in range(rows_n)]
    down = [(b, a) for a, b in up]

    def send(value, axis, count, bit):
        return lax.ppermute(value, axis, [(i, i ^ bit) for i in range(count)])

    def send_row(value, bit):
        return send(value, "row", rows_n, bit)

    def finish_cols(own, other):
        held = {0: own, cols_n // 2: other}
        bit = cols_n // 4
        while bit:
            held.update({q ^ bit: send(v, "col", cols_n, bit) for q, v in list(held.items())})
            bit //= 2
        return [held[q] for q in range(cols_n)]

    def send_far_col(value):
        return send(value, "col", cols_n, cols_n // 2)

    lanes = -(-2 * rows_n * tcols // LANES) * LANES
    note = pl.pallas_call(
        functools.partial(note_kernel, rows_n),
        out_shape=jax.ShapeDtypeStruct((1, cols_dev + lanes), jnp.float32),
        in_specs=[pl.BlockSpec(memory_space=pltpu.HBM)] * 3,
        out_specs=whole(),
        scratch_shapes=[
            pltpu.VMEM(flow.shape, flow.dtype),
            pltpu.SMEM(pattern.shape, pattern.dtype),
            pltpu.SMEM(keep.shape, keep.dtype),
            pltpu.SemaphoreType.DMA((3,)),
        ],
        compiler_params=pltpu.CompilerParams(vmem_limit_bytes=8 * tile * cols_dev * 2),
    )(flow, pattern, keep)

    def send_both(value, bit):
        pairs = [(r * cols_n + c, (r ^ bit) * cols_n + (c ^ (cols_n // 2))) for r in range(rows_n) for c in range(cols_n)]
        return lax.ppermute(value, ("row", "col"), pairs)

    ring = {0: flow}
    behind = ahead = flow
    bits = [1 << b for b in range(rows_n.bit_length() - 1)]
    bits[:2] = bits[1::-1]
    for s in range(1, half_ring):
        behind, ahead = lax.ppermute(behind, "row", up), lax.ppermute(ahead, "row", down)
        if s == 2:
            far = send_both(note, bits[1]) + send_far_col(note)
            near = note + send_row(note, bits[1])
            note = jnp.concatenate([near, far], axis=0)
        elif s <= len(bits):
            note = note + send_row(note, bits[s - 1])
        if s == 1:
            mine = send_far_col(flow)
            behind, ahead, note, mine = lax.optimization_barrier((behind, ahead, note, mine))
        else:
            behind, ahead, note = lax.optimization_barrier((behind, ahead, note))
        ring[s], ring[rows_n - s] = ahead, behind
        if s == quarter:
            mate = jnp.where(position % half_ring < quarter, ahead, behind)
            other_mate = send_far_col(mate)
    beside_note = send(note, "col", cols_n, 1)
    half = tile // 2
    top = lax.ppermute(behind[:half], "row", up)
    bottom = lax.ppermute(ahead[half:], "row", down)
    notes = [note[:1], beside_note[:1], note[1:], beside_note[1:]]
    note = note[:1]
    own_cols = finish_cols(flow, mine)
    mate_cols = finish_cols(mate, other_mate)

    blocks = [ring[o] for o in range(rows_n) if o != half_ring]
    col_block = pl.BlockSpec((tile, width), lambda j: (0, j), memory_space=pltpu.VMEM)
    wide_block = pl.BlockSpec((2 * tile, width), lambda j: (0, j), memory_space=pltpu.VMEM)
    half_block = pl.BlockSpec((half, width), lambda j: (0, j), memory_space=pltpu.VMEM)
    acc, left_last = pl.pallas_call(
        functools.partial(square_kernel, rows_n, cols_n, half_ring),
        grid=grid,
        out_shape=(
            jax.ShapeDtypeStruct((2 * tile, cols_dev), jnp.float32),
            jax.ShapeDtypeStruct((2 * tile, tile), jnp.bfloat16),
        ),
        in_specs=[col_block] * len(blocks) + [fixed(v.shape) for v in own_cols + mate_cols + notes],
        out_specs=(wide_block, fixed((2 * tile, tile))),
        scratch_shapes=[
            pltpu.VMEM((2 * tile, rows_n * tile), jnp.bfloat16),
            pltpu.VMEM((rows_n * tile, width), jnp.bfloat16),
            pltpu.VMEM((cols_n * tcols, rows_n, tile), jnp.float32),
        ],
        cost_estimate=pl.CostEstimate(
            flops=4 * tile * tile * rows_n * cols_dev, bytes_accessed=24 * tile * cols_dev, transcendentals=0
        ),
        compiler_params=pltpu.CompilerParams(vmem_limit_bytes=(20 if small else 60) * 1024 * 1024),
    )(*blocks, *own_cols, *mate_cols, *notes)

    inflated, totals = pl.pallas_call(
        functools.partial(inflate_kernel, rows_n, half_ring),
        grid=grid,
        out_shape=(
            jax.ShapeDtypeStruct((tile, cols_dev), jnp.float32),
            jax.ShapeDtypeStruct((1, cols_dev), jnp.float32),
        ),
        in_specs=[wide_block, fixed((2 * tile, tile)), half_block, half_block, fixed(note.shape)],
        out_specs=(col_block, pl.BlockSpec((1, width), lambda j: (0, j), memory_space=pltpu.VMEM)),
        scratch_shapes=[pltpu.VMEM((tile, width), jnp.bfloat16)],
        cost_estimate=pl.CostEstimate(
            flops=4 * tile * tile * cols_dev, bytes_accessed=16 * tile * cols_dev, transcendentals=0
        ),
        compiler_params=pltpu.CompilerParams(vmem_limit_bytes=16 * 1024 * 1024),
    )(acc, left_last, top, bottom, note)

    bit = 1
    while bit < half_ring:
        if 2 * bit < half_ring:
            across = send_row(totals, 3 * bit)
            totals = (totals + across) + (send_row(totals, bit) + send_row(totals, 2 * bit))
            bit *= 4
        else:
            totals = totals + send_row(totals, bit)
            bit *= 2
    return inflated * (rows_n * tile / totals)


def solution(mesh):
    return jax.shard_map(
        functools.partial(body, mesh.shape["row"], mesh.shape["col"]),
        mesh=mesh,
        in_specs=(P("row", "col"), P("row", "col"), P("row", "col")),
        out_specs=P("row", "col"),
        check_vma=False,
    )
```

```python
import functools

import jax
import jax.numpy as jnp
from jax import lax
from jax.experimental import pallas as pl
from jax.experimental.pallas import tpu as pltpu
from jax.sharding import PartitionSpec as P

LANES = 128


def ring_order(count):
    return list(range(0, count, 2)) + list(range(count - 1, 0, -2))


def ring_position(index, count):
    return jnp.where(index % 2 == 0, index // 2, count - 1 - index // 2)


def ring_member(position, count):
    position = lax.rem(position + count, count)
    return jnp.where(position < count // 2, 2 * position, 2 * (count - 1 - position) + 1)


def identity(tile):
    rows = lax.broadcasted_iota(jnp.int32, (tile, tile), 0)
    return (rows == lax.broadcasted_iota(jnp.int32, (tile, tile), 1)).astype(jnp.float32)


def lane(note, start, index):
    tail = note[:, start:]
    return jnp.sum(jnp.where(lax.broadcasted_iota(jnp.int32, tail.shape, 1) == index, tail, 0.0), axis=1, keepdims=True)


def mask_rows(note, start, rows_n, tcols, t, tile):
    tail = note[:, start:]
    shape = (rows_n, tail.shape[1])
    wanted = lax.broadcasted_iota(jnp.int32, shape, 0) * tcols + t
    chosen = jnp.where(lax.broadcasted_iota(jnp.int32, shape, 1) == wanted, tail, 0.0)
    return jnp.broadcast_to(jnp.sum(chosen, axis=1, keepdims=True), (rows_n, tile))


def note_kernel(rows_n, flow_hbm, pattern_hbm, keep_hbm, note_ref, flow_ref, pattern_ref, keep_ref, sems):
    pairs = ((flow_hbm, flow_ref), (pattern_hbm, pattern_ref), (keep_hbm, keep_ref))
    copies = [pltpu.make_async_copy(a, b, sems.at[i]) for i, (a, b) in enumerate(pairs)]
    for copy in copies:
        copy.start()
    for copy in copies:
        copy.wait()
    tile, cols_dev = flow_ref.shape
    tcols = cols_dev // tile
    row, col = lax.axis_index("row"), lax.axis_index("col")
    lanes = lax.broadcasted_iota(jnp.int32, (1, note_ref.shape[1] - cols_dev), 1)
    masks = jnp.zeros(lanes.shape, jnp.float32)
    for t in range(tcols):
        cut = slice(t * tile, (t + 1) * tile)
        loop = col * tcols + t == row
        listed = (pattern_ref[0, t] > 0).astype(jnp.float32)
        kept = jnp.logical_or(keep_ref[0, t] > 0, loop).astype(jnp.float32)
        sums = jnp.sum(flow_ref[:, cut].astype(jnp.float32), axis=0, keepdims=True)
        note_ref[:, cut] = sums * listed + loop.astype(jnp.float32)
        masks = jnp.where(lanes == row * tcols + t, listed, masks)
        masks = jnp.where(lanes == (rows_n + row) * tcols + t, kept, masks)
    note_ref[:, cols_dev:] = masks


def store_normalized(place, block, flag, inverse, is_diagonal):
    place[...] = (block[...].astype(jnp.float32) * (inverse * flag)).astype(jnp.bfloat16)

    @pl.when(is_diagonal)
    def _():
        base = block[...].astype(jnp.float32) * flag + identity(block.shape[0])
        place[...] = (base * inverse).astype(jnp.bfloat16)


def square_kernel(rows_n, cols_n, last, *refs):
    blocks, refs = refs[: rows_n - 1], refs[rows_n - 1 :]
    own_cols, refs = refs[:cols_n], refs[cols_n:]
    mate_cols, refs = refs[:cols_n], refs[cols_n:]
    notes, refs = refs[:cols_n], refs[cols_n:]
    acc_ref, left_last_ref, left, right, flags = refs
    step = pl.program_id(0)
    row, col = lax.axis_index("row"), lax.axis_index("col")
    position = ring_position(row, rows_n)
    mate = row ^ (rows_n // 2)
    tile, cols_dev = own_cols[0].shape
    tcols = cols_dev // tile
    width = acc_ref.shape[1]

    @pl.when(step == 0)
    def _():
        for q in range(cols_n):
            for t in range(tcols):
                flags[q * tcols + t] = mask_rows(notes[q], cols_dev, rows_n, tcols, t, tile)
        for q in range(cols_n):
            for t in range(tcols):
                cut = slice(t * tile, (t + 1) * tile)
                inverse = 1.0 / notes[q][:, cut]
                k = (col ^ q) * tcols + t
                slot = lax.rem(ring_position(k, rows_n) - position + rows_n, rows_n)
                lanes = pl.ds(pl.multiple_of(slot * tile, tile), tile)
                for half, cols, r in ((0, own_cols, row), (1, mate_cols, mate)):
                    flag = flags[q * tcols + t, pl.ds(r, 1), :]
                    place = left.at[half * tile : (half + 1) * tile, lanes]
                    store_normalized(place, cols[q].at[:, cut], flag, inverse, k == r)
        left_last_ref[...] = left[:, last * tile : (last + 1) * tile]

    slots = [s for s in range(rows_n) if s != last]
    for slot, block in zip(slots, blocks):
        r = ring_member(position + slot, rows_n)
        for t in range(width // tile):
            cut = slice(t * tile, (t + 1) * tile)
            tile_col = step * (width // tile) + t
            lanes = pl.ds(pl.multiple_of(tile_col * tile, tile), tile)
            place = right.at[slot * tile : (slot + 1) * tile, cut]
            flag = flags[tile_col, pl.ds(r, 1), :]
            store_normalized(place, block.at[:, cut], flag, 1.0 / notes[0][:, lanes], col * tcols + tile_col == r)
    group = 4
    pieces = [(a, min(a + group, last)) for a in range(0, last, group)]
    pieces += [(a, min(a + group, rows_n)) for a in range(last + 1, rows_n, group)]
    for number, (a, b) in enumerate(pieces):
        span = slice(a * tile, b * tile)
        product = jnp.dot(left[:, span], right[span, :], preferred_element_type=jnp.float32)
        acc_ref[...] = product if number == 0 else acc_ref[...] + product


def inflate_kernel(rows_n, last, acc_ref, left_ref, top_ref, bottom_ref, note_ref, out_ref, tot_ref, right):
    step = pl.program_id(0)
    row, col = lax.axis_index("row"), lax.axis_index("col")
    r = ring_member(ring_position(row, rows_n) + last, rows_n)
    tile, width = out_ref.shape
    per_step = width // tile
    tcols = per_step * pl.num_programs(0)
    cols_dev = tcols * tile
    half = top_ref.shape[0]
    for t in range(per_step):
        cut = slice(t * tile, (t + 1) * tile)
        tile_col = step * per_step + t
        flag = lane(note_ref, cols_dev, r * tcols + tile_col)
        inverse = 1.0 / note_ref[:, pl.ds(pl.multiple_of(tile_col * tile, tile), tile)]
        right[0:half, cut] = (top_ref[:, cut].astype(jnp.float32) * (inverse * flag)).astype(jnp.bfloat16)
        right[half:tile, cut] = (bottom_ref[:, cut].astype(jnp.float32) * (inverse * flag)).astype(jnp.bfloat16)

        @pl.when(col * tcols + tile_col == r)
        def _():
            eye = identity(tile)
            top = top_ref[:, cut].astype(jnp.float32) * flag + eye[0:half]
            bottom = bottom_ref[:, cut].astype(jnp.float32) * flag + eye[half:tile]
            right[0:half, cut] = (top * inverse).astype(jnp.bfloat16)
            right[half:tile, cut] = (bottom * inverse).astype(jnp.bfloat16)

    for t in range(per_step):
        cut = slice(t * tile, (t + 1) * tile)
        tile_col = step * per_step + t
        product = acc_ref[:, cut] + jnp.dot(left_ref[...], right[:, cut], preferred_element_type=jnp.float32)
        mine = product[0:tile] * lane(note_ref, cols_dev, (rows_n + row) * tcols + tile_col)
        mine = mine * mine
        out_ref[:, cut] = mine
        mate = row ^ (rows_n // 2)
        other = product[tile : 2 * tile] * lane(note_ref, cols_dev, (rows_n + mate) * tcols + tile_col)
        tot_ref[:, cut] = jnp.sum(mine + other * other, axis=0, keepdims=True)


def scale_kernel(order_total, parts, inflated_ref, totals_ref, out_hbm, scaled, sems):
    factor = order_total / totals_ref[...]
    size = inflated_ref.shape[0] // parts
    copies = []
    for part in range(parts):
        rows = pl.ds(part * size, size)
        scaled[rows, :] = inflated_ref[rows, :] * factor
        copies.append(pltpu.make_async_copy(scaled.at[rows, :], out_hbm.at[rows, :], sems.at[part]))
        copies[-1].start()
    for copy in copies:
        copy.wait()


def whole():
    return pl.BlockSpec(memory_space=pltpu.VMEM)


def fixed(shape):
    return pl.BlockSpec(shape, lambda j: (0, 0), memory_space=pltpu.VMEM)


def body(rows_n, cols_n, flow, pattern, keep):
    tile, cols_dev = flow.shape
    tcols = pattern.shape[1]
    row = lax.axis_index("row")
    position = ring_position(row, rows_n)
    half_ring, quarter = rows_n // 2, rows_n // 4
    width = min(cols_dev, 2 * tile)
    grid = (cols_dev // width,)
    small = rows_n * tile <= 2048

    order = ring_order(rows_n)
    up = [(order[i], order[(i + 1) % rows_n]) for i in range(rows_n)]
    down = [(b, a) for a, b in up]

    def send(value, axis, count, bit):
        return lax.ppermute(value, axis, [(i, i ^ bit) for i in range(count)])

    def send_row(value, bit):
        return send(value, "row", rows_n, bit)

    def finish_cols(own, other):
        held = {0: own, cols_n // 2: other}
        bit = cols_n // 4
        while bit:
            held.update({q ^ bit: send(v, "col", cols_n, bit) for q, v in list(held.items())})
            bit //= 2
        return [held[q] for q in range(cols_n)]

    def send_far_col(value):
        return send(value, "col", cols_n, cols_n // 2)

    lanes = -(-2 * rows_n * tcols // LANES) * LANES
    note = pl.pallas_call(
        functools.partial(note_kernel, rows_n),
        out_shape=jax.ShapeDtypeStruct((1, cols_dev + lanes), jnp.float32),
        in_specs=[pl.BlockSpec(memory_space=pltpu.HBM)] * 3,
        out_specs=whole(),
        scratch_shapes=[
            pltpu.VMEM(flow.shape, flow.dtype),
            pltpu.SMEM(pattern.shape, pattern.dtype),
            pltpu.SMEM(keep.shape, keep.dtype),
            pltpu.SemaphoreType.DMA((3,)),
        ],
        compiler_params=pltpu.CompilerParams(vmem_limit_bytes=8 * tile * cols_dev * 2),
    )(flow, pattern, keep)

    def send_both(value, bit):
        pairs = [(r * cols_n + c, (r ^ bit) * cols_n + (c ^ (cols_n // 2))) for r in range(rows_n) for c in range(cols_n)]
        return lax.ppermute(value, ("row", "col"), pairs)

    ring = {0: flow}
    behind = ahead = flow
    bits = [1 << b for b in range(rows_n.bit_length() - 1)]
    bits[:2] = bits[1::-1]
    for s in range(1, half_ring):
        behind, ahead = lax.ppermute(behind, "row", up), lax.ppermute(ahead, "row", down)
        if s == 2:
            far = send_both(note, bits[1]) + send_far_col(note)
            near = note + send_row(note, bits[1])
            note = jnp.concatenate([near, far], axis=0)
        elif s <= len(bits):
            note = note + send_row(note, bits[s - 1])
        if s == 1:
            mine = send_far_col(flow)
            behind, ahead, note, mine = lax.optimization_barrier((behind, ahead, note, mine))
        else:
            behind, ahead, note = lax.optimization_barrier((behind, ahead, note))
        ring[s], ring[rows_n - s] = ahead, behind
        if s == quarter:
            mate = jnp.where(position % half_ring < quarter, ahead, behind)
            other_mate = send_far_col(mate)
    beside_note = send(note, "col", cols_n, 1)
    half = tile // 2
    top = lax.ppermute(behind[:half], "row", up)
    bottom = lax.ppermute(ahead[half:], "row", down)
    notes = [note[:1], beside_note[:1], note[1:], beside_note[1:]]
    note = note[:1]
    own_cols = finish_cols(flow, mine)
    mate_cols = finish_cols(mate, other_mate)

    blocks = [ring[o] for o in range(rows_n) if o != half_ring]
    col_block = pl.BlockSpec((tile, width), lambda j: (0, j), memory_space=pltpu.VMEM)
    wide_block = pl.BlockSpec((2 * tile, width), lambda j: (0, j), memory_space=pltpu.VMEM)
    half_block = pl.BlockSpec((half, width), lambda j: (0, j), memory_space=pltpu.VMEM)
    acc, left_last = pl.pallas_call(
        functools.partial(square_kernel, rows_n, cols_n, half_ring),
        grid=grid,
        out_shape=(
            jax.ShapeDtypeStruct((2 * tile, cols_dev), jnp.float32),
            jax.ShapeDtypeStruct((2 * tile, tile), jnp.bfloat16),
        ),
        in_specs=[col_block] * len(blocks) + [fixed(v.shape) for v in own_cols + mate_cols + notes],
        out_specs=(wide_block, fixed((2 * tile, tile))),
        scratch_shapes=[
            pltpu.VMEM((2 * tile, rows_n * tile), jnp.bfloat16),
            pltpu.VMEM((rows_n * tile, width), jnp.bfloat16),
            pltpu.VMEM((cols_n * tcols, rows_n, tile), jnp.float32),
        ],
        cost_estimate=pl.CostEstimate(
            flops=4 * tile * tile * rows_n * cols_dev, bytes_accessed=24 * tile * cols_dev, transcendentals=0
        ),
        compiler_params=pltpu.CompilerParams(vmem_limit_bytes=(20 if small else 60) * 1024 * 1024),
    )(*blocks, *own_cols, *mate_cols, *notes)

    inflated, totals = pl.pallas_call(
        functools.partial(inflate_kernel, rows_n, half_ring),
        grid=grid,
        out_shape=(
            jax.ShapeDtypeStruct((tile, cols_dev), jnp.float32),
            jax.ShapeDtypeStruct((1, cols_dev), jnp.float32),
        ),
        in_specs=[wide_block, fixed((2 * tile, tile)), half_block, half_block, fixed(note.shape)],
        out_specs=(col_block, pl.BlockSpec((1, width), lambda j: (0, j), memory_space=pltpu.VMEM)),
        scratch_shapes=[pltpu.VMEM((tile, width), jnp.bfloat16)],
        cost_estimate=pl.CostEstimate(
            flops=4 * tile * tile * cols_dev, bytes_accessed=16 * tile * cols_dev, transcendentals=0
        ),
        compiler_params=pltpu.CompilerParams(vmem_limit_bytes=16 * 1024 * 1024),
    )(acc, left_last, top, bottom, note)

    bit = 1
    while bit < half_ring:
        if 2 * bit < half_ring:
            across = send_row(totals, 3 * bit)
            totals = (totals + across) + (send_row(totals, bit) + send_row(totals, 2 * bit))
            bit *= 4
        else:
            totals = totals + send_row(totals, bit)
            bit *= 2
    parts = 4
    return pl.pallas_call(
        functools.partial(scale_kernel, float(rows_n * tile), parts),
        out_shape=jax.ShapeDtypeStruct((tile, cols_dev), jnp.float32),
        in_specs=[whole(), whole()],
        out_specs=pl.BlockSpec(memory_space=pl.ANY),
        scratch_shapes=[pltpu.VMEM((tile, cols_dev), jnp.float32), pltpu.SemaphoreType.DMA((parts,))],
        compiler_params=pltpu.CompilerParams(vmem_limit_bytes=8 * 4 * tile * cols_dev),
    )(inflated, totals)


def solution(mesh):
    return jax.shard_map(
        functools.partial(body, mesh.shape["row"], mesh.shape["col"]),
        mesh=mesh,
        in_specs=(P("row", "col"), P("row", "col"), P("row", "col")),
        out_specs=P("row", "col"),
        check_vma=False,
    )
```
